256 devices in a mesh: dom: 16 (over z_hi, y), rep: 16 (over x, z_lo, core).
Axes of the slice: x: 4, y: 4, z: 8 (z_hi: 4, z_lo: 2; z = z_hi * 2 + z_lo), core: 2. Of those that a mesh axis runs over, the one named last changes fastest.
Arguments:
- grad_codes: int32 [14336, 4096], P('dom', 'rep'), may hold values from -127 to 127
- grad_scales: float32 [32, 14336], P('rep', 'dom'), may hold values from 0.004 to 0.04
- weight_codes: int32 [4096, 14336], P('dom', 'rep'), may hold values from -127 to 127
- weight_scales: float32 [32, 14336], P('dom', 'rep'), may hold values from 7e-05 to 0.0007
- gate_preact: bfloat16 [14336, 14336], P('dom', 'rep'), may hold values from -6 to 6
- up_preact: bfloat16 [14336, 14336], P('dom', 'rep'), may hold values from -6 to 6
Outputs:
- gate_grad: bfloat16 [14336, 14336], P('dom', 'rep')
- up_grad: bfloat16 [14336, 14336], P('dom', 'rep')
- weight_grad: float32 [4096, 14336], P('dom', 'rep')
The draws below stay inside these ranges and needn't reach their ends.
All inputs are finite; a program needn't handle non-finite values.
Results may differ from the reference program's by a relative error of at most 0.0058.
Values may be sent and summed in bfloat16 or wider, within the bound.
No kernel may reach another device: no remote copies, remote signals or barrier semaphores. Data moves between devices by JAX's collectives and lax.ppermute only.
A program may use at most 128 MiB of HBM per device.

```python
import math
import jax
import jax.numpy as jnp
from jax import lax

D = 4096
FF = 14336
QB = 128
TOKENS = 14336


def with_ends(array, rng, least, high):
    index_at = [jax.random.randint(jax.random.fold_in(rng, axis), (), 0, length) for axis, length in enumerate(array.shape)]
    main_axis = array.shape.index(max(array.shape))
    next_to = index_at[:main_axis] + [(index_at[main_axis] + 1) % array.shape[main_axis]] + index_at[main_axis + 1:]
    return array.at[tuple(index_at)].set(least).at[tuple(next_to)].set(high)


def levels(key, dims, split, smallest, high):
    def one(dim, parts):
        steps = jax.random.uniform(jax.random.fold_in(jax.random.fold_in(key, 6), dim), (parts,), jnp.float32, smallest / len(split), high / len(split))
        return jnp.repeat(jnp.exp(steps), dims[dim] // parts).reshape((-1,) + (1,) * (len(dims) - dim - 1))

    level = one(*split[0])
    for cut in split[1:]:
        level = level * one(*cut)
    return level


def bell_draw(rng, shape, scale, reach, cuts=(), kind=jnp.bfloat16):
    values = jax.random.normal(rng, shape, jnp.float32) * scale
    if len(cuts) > 0:
        values = levels(rng, shape, cuts, -0.22, 0.18) * values
    return jnp.clip(values, min=-reach, max=reach).astype(kind)


def setup_inputs(seed: int = 0) -> dict:
    splits = jax.random.split(jax.random.key(seed), 7)
    return {
        "grad_codes": with_ends(jax.random.randint(splits[0], (TOKENS, D), -127, 128), jax.random.fold_in(splits[0], 1), -127, 127).astype(jnp.int32),
        "grad_scales": jnp.clip(jnp.exp(math.log(0.04) - 2.30258502 * jax.random.uniform(splits[1], (D // QB, TOKENS), jnp.float32) ** levels(splits[1], (D // QB, TOKENS), ((0, 16), (1, 16)), -0.2, 0.2)), 0.004, 0.04),
        "weight_codes": with_ends(jax.random.randint(splits[2], (D, FF), -127, 128), jax.random.fold_in(splits[2], 1), -127, 127).astype(jnp.int32),
        "weight_scales": jnp.clip(jnp.exp(math.log(0.0007) - 2.30258503 * jax.random.uniform(splits[3], (D // QB, FF), jnp.float32) ** levels(splits[3], (D // QB, FF), ((0, 16), (1, 16)), -0.2, 0.2)), 7.000000186963007e-05, 0.0007),
        "gate_preact": bell_draw(splits[4], (TOKENS, FF), 1.0, 6.0, ((0, 16), (1, 16))),
        "up_preact": bell_draw(splits[5], (TOKENS, FF), 1.0, 6.0, ((0, 16), (1, 16))),
    }


def expand_grad(int_codes, block_scales):
    rows = int_codes.shape[0]
    blocks = block_scales.shape[0]
    values = int_codes.astype(jnp.float32).reshape(rows, blocks, QB) * jnp.transpose(block_scales)[:, :, None]
    return values.reshape(rows, blocks * QB).astype(jnp.bfloat16)

def expand_weight(int_codes, block_scales):
    blocks = block_scales.shape[0]
    width = int_codes.shape[1]
    values = int_codes.astype(jnp.float32).reshape(blocks, QB, width) * block_scales[:, None, :]
    return values.reshape(blocks * QB, width).astype(jnp.bfloat16)

def reference(grad_codes, grad_scales, weight_codes, weight_scales, gate_preact, up_preact):
    upstream = expand_grad(grad_codes, grad_scales)
    weight = expand_weight(weight_codes, weight_scales)
    hidden_grad = jnp.dot(upstream, weight, preferred_element_type=jnp.float32)
    gate_val = gate_preact.astype(jnp.float32)
    up_val = up_preact.astype(jnp.float32)
    squash = jax.nn.sigmoid(gate_val)
    swish = gate_val * squash
    hidden = (swish * up_val).astype(jnp.bfloat16)
    up_grad = (hidden_grad * swish).astype(jnp.bfloat16)
    gate_grad = (hidden_grad * up_val * squash * (1.0 + gate_val * (1.0 - squash))).astype(jnp.bfloat16)
    weight_grad = lax.dot_general(upstream, hidden, (((0,), (0,)), ((), ())), preferred_element_type=jnp.float32)
    return (gate_grad, up_grad, weight_grad)
```

```python
import functools

import jax
import jax.numpy as jnp
from jax import lax
from jax.experimental import pallas as pl
from jax.experimental.pallas import tpu as pltpu
from jax.sharding import Mesh
from jax.sharding import PartitionSpec as P

QB = 128
VMEM_LIMIT = 50 * 1024 * 1024
ANY = pl.BlockSpec(memory_space=pl.ANY)
SMEM = pl.BlockSpec(memory_space=pltpu.SMEM)
VMEM = pl.BlockSpec(memory_space=pltpu.VMEM)
SIZE = {"zh": 4, "y": 4, "x": 4, "zl": 2, "core": 2}
F32, BF16 = jnp.float32, jnp.bfloat16


def send(v, axis, step):
    n = SIZE[axis]
    return lax.ppermute(v, axis, [(i, (i + step) % n) for i in range(n)])


def expand_weight(codes, scales):
    blocks, width = scales.shape
    values = codes.astype(F32).reshape(blocks, QB, width) * scales[:, None, :]
    return values.reshape(blocks * QB, width).astype(BF16)


def expand_grad_kernel(codes, scales, out):
    rows = codes.shape[0]
    for b in range(scales.shape[0]):
        s = jnp.broadcast_to(scales[b : b + 1, :], (QB, rows)).T
        cols = slice(b * QB, (b + 1) * QB)
        out[:, cols] = (codes[:, cols].astype(F32) * s).astype(BF16)


def expand_grad(codes, scales):
    return pl.pallas_call(
        expand_grad_kernel,
        out_shape=jax.ShapeDtypeStruct(codes.shape, BF16),
        in_specs=[VMEM, VMEM],
        out_specs=VMEM,
        compiler_params=pltpu.CompilerParams(vmem_limit_bytes=VMEM_LIMIT),
    )(codes, scales)


def halves(v):
    n = v.shape[0] // 2
    return v[:n], v[n:]


def gather_upstream(own):
    pieces = []
    half = own.shape[0] // 2
    for dzl in range(2):
        base = own if dzl == 0 else send(own, "zl", 1)
        left, right = send(base, "x", 1), send(base, "x", -1)
        far0 = send(halves(left)[0], "x", 1)
        far1 = send(halves(right)[1], "x", -1)
        pieces += [(0, dzl, 0, base), (3, dzl, 0, left), (1, dzl, 0, right), (2, dzl, 0, far0), (2, dzl, half, far1)]
    out = []
    for dx, dzl, row, v in pieces:
        out.append((dx, dzl, 0, row, v))
        out.append((dx, dzl, 1, row, send(v, "core", 1)))
    return out


def gather_weight(own):
    half = own.shape[0] // 2
    pieces = [(0, 0, 0, own)]
    up, down = send(own, "zh", 1), send(own, "zh", -1)
    left, right = send(own, "y", 1), send(own, "y", -1)
    far0 = send(halves(left)[0], "y", 1)
    far1 = send(halves(right)[1], "y", -1)
    pieces += [(0, 3, 0, left), (0, 1, 0, right), (0, 2, 0, far0), (0, 2, half, far1)]
    pieces += [(3, 0, 0, up), (1, 0, 0, down)]
    for dz, v in ((3, up), (1, down)):
        pieces += [(dz, 3, 0, send(v, "y", 1)), (dz, 1, 0, send(v, "y", -1))]
    zfar0 = send(halves(up)[0], "zh", 1)
    zfar1 = send(halves(down)[1], "zh", -1)
    pieces += [(2, 0, 0, zfar0), (2, 0, half, zfar1)]
    l0, l1 = send(zfar0, "y", 1), send(zfar1, "y", 1)
    r0, r1 = send(zfar0, "y", -1), send(zfar1, "y", -1)
    pieces += [(2, 3, 0, l0), (2, 3, half, l1), (2, 1, 0, r0), (2, 1, half, r1)]
    pieces += [(2, 2, 0, send(l0, "y", 1)), (2, 2, half, send(r1, "y", -1))]
    for row, v in ((0, far0), (half, far1)):
        pieces += [(3, 2, row, send(v, "zh", 1)), (1, 2, row, send(v, "zh", -1))]
    return pieces


def partial_kernel(jz, metas, out_jy, at, hidden, *refs):
    n = len(metas)
    pieces, outs, held, sem = refs[:n], refs[n : n + len(out_jy)], refs[-2], refs[-1]
    zh, y, x, zl, core = [at[i] for i in range(5)]
    want = lax.rem(zh + jz + 4 - x, 4)

    def copies(dx):
        found = []
        for (px, pzl, pcore, row, rows), ref in zip(metas, pieces):
            if px == dx:
                slot = 2 * jnp.bitwise_xor(zl, pzl) + jnp.bitwise_xor(core, pcore)
                found.append(pltpu.make_async_copy(ref, held.at[slot, pl.ds(row, rows)], sem))
        return found

    for dx in range(4):

        @pl.when(want == dx)
        def _():
            for c in copies(dx):
                c.start()
            for c in copies(dx):
                c.wait()

    for jy, out in zip(out_jy, outs):
        u = held[lax.rem(y + jy, 4)]
        r = lax.dot_general(u, hidden[...], (((0,), (0,)), ((), ())), preferred_element_type=F32)
        out[...] = r.astype(out.dtype)


def partials(jz, at, hidden, upstream, kinds):
    metas = [(dx, dzl, dcore, row, v.shape[0]) for dx, dzl, dcore, row, v in upstream]
    arrays = [p[-1] for p in upstream]
    rows = hidden.shape[0]
    width = arrays[0].shape[1]
    jys = list(kinds)
    flops = 2 * rows * hidden.shape[1] * width * len(jys)
    return pl.pallas_call(
        functools.partial(partial_kernel, jz, metas, jys),
        out_shape=[jax.ShapeDtypeStruct((width, hidden.shape[1]), kinds[jy]) for jy in jys],
        in_specs=[SMEM, VMEM] + [ANY] * len(arrays),
        out_specs=[VMEM] * len(jys),
        scratch_shapes=[pltpu.VMEM((4, rows, width), BF16), pltpu.SemaphoreType.DMA],
        compiler_params=pltpu.CompilerParams(vmem_limit_bytes=VMEM_LIMIT),
        cost_estimate=pl.CostEstimate(flops=flops, bytes_accessed=8 * 1024 * 1024, transcendentals=0),
    )(at, hidden, *arrays)


TILE = 448


def hidden_kernel(umetas, wmetas, at, *refs):
    nu, nw = len(umetas), len(wmetas)
    us, ws = refs[:nu], refs[nu : nu + nw]
    gate, up, gate_out, up_out, uheld, wheld, sem = refs[nu + nw :]
    zh, y, x, zl, core = [at[i] for i in range(5)]

    def copies():
        for (dx, dzl, dcore, row, rows), ref in zip(umetas, us):
            f = lax.rem(x + dx, 4) * 4 + 2 * jnp.bitwise_xor(zl, dzl) + jnp.bitwise_xor(core, dcore)
            width = ref.shape[1]
            yield pltpu.make_async_copy(
                ref, uheld.at[pl.ds(row, rows), pl.ds(pl.multiple_of(f * width, width), width)], sem
            )
        for (dz, dy, row, rows), ref in zip(wmetas, ws):
            f = lax.rem(zh + dz, 4) * 4 + lax.rem(y + dy, 4)
            depth = uheld.shape[1] // 16
            yield pltpu.make_async_copy(ref, wheld.at[pl.ds(pl.multiple_of(f * depth + row, row or depth), rows)], sem)

    for c in copies():
        c.start()
    for c in copies():
        c.wait()

    @pl.loop(0, gate.shape[0] // TILE)
    def _(i):
        at_rows = pl.ds(pl.multiple_of(i * TILE, TILE), TILE)
        grad = jnp.dot(uheld[at_rows, :], wheld[...], preferred_element_type=F32)
        g = gate[at_rows, :].astype(F32)
        u = up[at_rows, :].astype(F32)
        s = 1.0 / (1.0 + jnp.exp(-g))
        up_out[at_rows, :] = (grad * (g * s)).astype(BF16)
        gate_out[at_rows, :] = (grad * u * s * (1.0 + g * (1.0 - s))).astype(BF16)


def hidden_grads(at, upstream, weight, gate, up):
    umetas = [(dx, dzl, dcore, row, v.shape[0]) for dx, dzl, dcore, row, v in upstream]
    wmetas = [(dz, dy, row, v.shape[0]) for dz, dy, row, v in weight]
    arrays = [p[-1] for p in upstream] + [p[-1] for p in weight]
    depth = 16 * upstream[0][-1].shape[1]
    shape = jax.ShapeDtypeStruct(gate.shape, BF16)
    return pl.pallas_call(
        functools.partial(hidden_kernel, umetas, wmetas),
        out_shape=[shape, shape],
        in_specs=[SMEM] + [ANY] * len(arrays) + [VMEM, VMEM],
        out_specs=[VMEM, VMEM],
        scratch_shapes=[
            pltpu.VMEM((gate.shape[0], depth), BF16),
            pltpu.VMEM((depth, gate.shape[1]), BF16),
            pltpu.SemaphoreType.DMA,
        ],
        compiler_params=pltpu.CompilerParams(vmem_limit_bytes=VMEM_LIMIT),
        cost_estimate=pl.CostEstimate(
            flops=2 * gate.shape[0] * gate.shape[1] * depth, bytes_accessed=24 * 1024 * 1024, transcendentals=0
        ),
    )(at, *arrays, gate, up)


def add(*terms):
    return functools.reduce(jnp.add, [t.astype(F32) for t in terms])


def body(grad_codes, grad_scales, weight_codes, weight_scales, gate_preact, up_preact):
    at = jnp.stack([lax.axis_index(a) for a in ("zh", "y", "x", "zl", "core")]).astype(jnp.int32)
    weight = gather_weight(expand_weight(weight_codes, weight_scales))
    upstream = gather_upstream(expand_grad(grad_codes, grad_scales))

    g = gate_preact.astype(F32)
    hidden = (g * jax.nn.sigmoid(g) * up_preact.astype(F32)).astype(BF16)

    p1 = dict(zip((2, 1, 3, 0), partials(1, at, hidden, upstream, {2: BF16, 1: BF16, 3: BF16, 0: F32})))
    p3 = dict(zip((2, 1, 3, 0), partials(3, at, hidden, upstream, {2: BF16, 1: BF16, 3: BF16, 0: F32})))
    p2 = dict(zip((2, 1, 3, 0), partials(2, at, hidden, upstream, {2: BF16, 1: F32, 3: F32, 0: F32})))
    p0 = dict(zip((2, 1, 3, 0), partials(0, at, hidden, upstream, {2: F32, 1: F32, 3: F32, 0: F32})))

    def along_y(p, far):
        if far is None:
            return add(p[0], send(p[1], "y", 1), send(p[3], "y", -1))
        a, b = halves(far)
        a, b = send(a, "y", 1), send(b, "y", -1)
        n = a.shape[0]
        to_right = jnp.concatenate([add(p[1][:n], a), p[1][n:]]).astype(BF16)
        to_left = jnp.concatenate([p[3][:n], add(p[3][n:], b)]).astype(BF16)
        return add(p[0], send(to_right, "y", 1), send(to_left, "y", -1))

    m1, m3 = send(p1[2], "zh", 1), send(p3[2], "zh", -1)
    c2 = along_y(p2, p2[2]).astype(BF16)
    c1, c3 = along_y(p1, None), along_y(p3, None)
    a, b = halves(c2)
    a, b = send(a, "zh", 1), send(b, "zh", -1)
    n = a.shape[0]
    up_sum = jnp.concatenate([add(c1[:n], a), c1[n:]]).astype(BF16)
    down_sum = jnp.concatenate([c3[:n], add(c3[n:], b)]).astype(BF16)
    c0 = along_y(p0, add(p0[2], m1, m3).astype(BF16))
    weight_grad = add(c0, send(up_sum, "zh", 1), send(down_sum, "zh", -1))

    gate_grad, up_grad = hidden_grads(at, upstream, weight, gate_preact, up_preact)
    return (gate_grad, up_grad, weight_grad)


def solution(mesh):
    fine = Mesh(mesh.devices.reshape(tuple(SIZE.values())), tuple(SIZE))
    dom, rep = ("zh", "y"), ("x", "zl", "core")
    in_specs = (P(dom, rep), P(rep, dom), P(dom, rep), P(dom, rep), P(dom, rep), P(dom, rep))
    out_specs = (P(dom, rep), P(dom, rep), P(dom, rep))
    return jax.shard_map(body, mesh=fine, in_specs=in_specs, out_specs=out_specs, check_vma=False)
```

```python
import functools

import jax
import jax.numpy as jnp
from jax import lax
from jax.experimental import pallas as pl
from jax.experimental.pallas import tpu as pltpu
from jax.sharding import Mesh
from jax.sharding import PartitionSpec as P

QB = 128
VMEM_LIMIT = 44 * 1024 * 1024
SMALL = 16 * 1024 * 1024
HBM = pl.BlockSpec(memory_space=pltpu.HBM)
SMEM = pl.BlockSpec(memory_space=pltpu.SMEM)
VMEM = pl.BlockSpec(memory_space=pltpu.VMEM)
SIZE = {"zh": 4, "y": 4, "x": 4, "zl": 2, "core": 2}
F32, BF16 = jnp.float32, jnp.bfloat16


def send(v, axis, step):
    n = SIZE[axis]
    return lax.ppermute(v, axis, [(i, (i + step) % n) for i in range(n)])


def call(kernel, shapes, in_specs, args, token=None, scratch=(), flops=0, moved=1 << 20, limit=SMALL, out_space=VMEM):
    tokens = () if token is None else (token,)
    n, m = len(args), len(shapes)

    def run(*refs):
        ins, rest = refs[:n], refs[n + len(tokens) :]
        rest[m][...] = jnp.zeros((8, 128), F32)
        kernel(*ins, *rest[:m], *rest[m + 1 :])

    out = pl.pallas_call(
        run,
        out_shape=[*shapes, array((8, 128), F32)],
        in_specs=[*in_specs, *[HBM] * len(tokens)],
        out_specs=[out_space] * m + [VMEM],
        scratch_shapes=list(scratch),
        compiler_params=pltpu.CompilerParams(vmem_limit_bytes=limit),
        cost_estimate=pl.CostEstimate(flops=flops, bytes_accessed=moved, transcendentals=0),
    )(*args, *tokens)
    return out[:-1], out[-1]


def array(shape, dtype):
    return jax.ShapeDtypeStruct(shape, dtype)


def expand_kernel(codes, scales, grad_codes, grad_scales, out, grad_out):
    for b in range(scales.shape[0]):
        rows = slice(b * QB, (b + 1) * QB)
        out[rows, :] = (codes[rows, :].astype(F32) * scales[b : b + 1, :]).astype(BF16)
        grad_out[rows, :] = (grad_codes[:, rows].astype(F32).T * grad_scales[b : b + 1, :]).astype(BF16)


def hidden_unit_kernel(gate, up, out):
    g = gate[...].astype(F32)
    out[...] = (g * (1.0 / (1.0 + jnp.exp(-g))) * up[...].astype(F32)).astype(BF16)


def send_split(v, axis):
    n = SIZE[axis]
    return lax.ppermute(v, (axis, "core"), [(2 * i + c, 2 * ((i + 1 - 2 * c) % n) + c) for i in range(n) for c in range(2)])


ZH, Y, X, ZL, CORE = range(5)


def join_kernel(a, b, out):
    n = a.shape[0]
    out[:n, :] = a[...]
    out[n:, :] = b[...]


def gather_upstream(mine, token):
    depth, width = mine.shape
    pieces = []
    for zl, base in enumerate((mine, send(mine, "zl", 1))):
        swapped = send(base, "core", 1)
        (pair,), _ = call(join_kernel, [array((2 * depth, width), BF16)], [VMEM] * 2, (base, swapped), token)
        near = send_split(pair, "x")
        token = near
        other = send(near, "core", 1)
        far = send_split(near[:depth], "x")
        pieces += [(0, zl, 0, 0, pair), (0, zl, 1, depth, pair), (1, zl, 0, 0, near), (1, zl, 1, depth, near)]
        pieces += [(2, zl, 1, 0, other), (2, zl, 0, depth, other), (3, zl, 0, 0, far), (3, zl, 1, 0, send(far, "core", 1))]
    return pieces


def x_away(at, kind):
    return (0, 3 - 2 * at[CORE], 1 + 2 * at[CORE], 2)[kind]


def partial_kernel(plan, metas, at, hidden, *refs):
    n = len(metas)
    m = len(plan)
    pieces, outs, done = refs[:n], refs[n : n + m], refs[n + m : n + 2 * m]
    held, sems, out_sems = refs[n + 2 * m :]
    blocks = [b for group in plan for b in group]
    depth = held.shape[1]

    for i, (jz, jy) in enumerate(blocks):
        away, owner = lax.rem(at[ZH] + jz + 4 - at[X], 4), lax.rem(at[Y] + jy, 4)
        zl, core = jnp.bitwise_xor(lax.div(owner, 2), at[ZL]), jnp.bitwise_xor(lax.rem(owner, 2), at[CORE])
        for (kind, pzl, pcore, row), ref in zip(metas, pieces):

            @pl.when((away == x_away(at, kind)) & (zl == pzl) & (core == pcore))
            def _():
                pltpu.make_async_copy(ref.at[pl.ds(row, depth)], held.at[i], sems.at[i]).start()

    copies = []
    for group, out, total in zip(plan, outs, done):
        for k in range(len(group)):
            i = len(copies)
            pltpu.make_async_copy(pieces[0].at[pl.ds(0, depth)], held.at[i], sems.at[i]).wait()
            r = jnp.dot(held[i], hidden[...], preferred_element_type=F32)
            rows = pl.ds(k * depth, depth)
            total[rows, :] = r.astype(out.dtype)
            copies.append(pltpu.make_async_copy(total.at[rows], out.at[rows], out_sems.at[i]))
            copies[-1].start()
    for c in copies:
        c.wait()


def partials(at, hidden, upstream, plan, dtypes, token):
    depth = upstream[0][-1].shape[0] // 2
    width = hidden.shape[1]
    n = sum(map(len, plan))
    shapes = [array((len(g) * depth, width), t) for g, t in zip(plan, dtypes)]
    return call(
        functools.partial(partial_kernel, plan, [p[:4] for p in upstream]),
        shapes,
        [SMEM, VMEM] + [HBM] * len(upstream),
        (at, hidden, *[p[-1] for p in upstream]),
        token,
        [pltpu.VMEM(t.shape, t.dtype) for t in shapes]
        + [pltpu.VMEM((n, depth, hidden.shape[0]), BF16), pltpu.SemaphoreType.DMA((n,)), pltpu.SemaphoreType.DMA((n,))],
        2 * hidden.shape[0] * width * depth * n,
        4 * 1024 * 1024,
        24 * 1024 * 1024,
        HBM,
    )


TILE = 448


def hidden_kernel(metas, at, weight, gate, up, *refs):
    n = len(metas)
    pieces = refs[:n]
    gate_out, up_out, uheld, wheld, sem = refs[n:]
    depth = uheld.shape[0] // 16

    def copies():
        yield pltpu.make_async_copy(weight, wheld, sem)
        for (kind, zl, core, row), ref in zip(metas, pieces):
            x = lax.rem(at[X] + x_away(at, kind), 4)
            f = 4 * x + 2 * jnp.bitwise_xor(at[ZL], zl) + jnp.bitwise_xor(at[CORE], core)
            rows = pl.ds(pl.multiple_of(f * depth, depth), depth)
            yield pltpu.make_async_copy(ref.at[pl.ds(row, depth)], uheld.at[rows], sem)

    for c in copies():
        c.start()
    for c in copies():
        c.wait()

    for i in range(gate.shape[0] // TILE):
        rows = slice(i * TILE, (i + 1) * TILE)
        grad = lax.dot_general(uheld[:, rows], wheld[...], (((0,), (0,)), ((), ())), preferred_element_type=F32)
        g = gate[rows, :].astype(F32)
        u = up[rows, :].astype(F32)
        s = 1.0 / (1.0 + jnp.exp(-g))
        up_out[rows, :] = (grad * (g * s)).astype(BF16)
        gate_out[rows, :] = (grad * u * s * (1.0 + g * (1.0 - s))).astype(BF16)


def hidden_grads(at, upstream, weight, gate, up, token):
    return call(
        functools.partial(hidden_kernel, [p[:4] for p in upstream]),
        [array(gate.shape, BF16)] * 2,
        [SMEM, HBM, VMEM, VMEM] + [HBM] * len(upstream),
        (at, weight, gate, up, *[p[-1] for p in upstream]),
        token,
        [pltpu.VMEM(weight.shape, BF16), pltpu.VMEM(weight.shape, BF16), pltpu.SemaphoreType.DMA],
        2 * gate.shape[0] * gate.shape[1] * weight.shape[0],
        20 * 1024 * 1024,
        VMEM_LIMIT,
    )


def spread_kernel(at, right, left, far, to_right, to_left):
    to_right[...] = right[...].astype(BF16)
    to_left[...] = left[...].astype(BF16)

    @pl.when(at[CORE] == 0)
    def _():
        to_right[...] = (right[...] + far[...].astype(F32)).astype(BF16)

    @pl.when(at[CORE] != 0)
    def _():
        to_left[...] = (left[...] + far[...].astype(F32)).astype(BF16)


def spread(at, right, left, far, token):
    return call(spread_kernel, [array(right.shape, BF16)] * 2, [SMEM, VMEM, VMEM, VMEM], (at, right, left, far), token)


def sum_kernel(first, *refs):
    out = refs[-1]
    rows = out.shape[0]
    total = 0.0
    for start, ref in zip(first, refs):
        total = total + ref[start : start + rows, :].astype(F32)
    out[...] = total.astype(out.dtype)


def sums_kernel(at, here, right, left, far, up, down):
    n = up.shape[0]
    far = far[...].astype(F32)
    total = here[...] + right[...].astype(F32) + left[...].astype(F32)
    up[...] = jnp.where(at[CORE] == 0, total[:n] + far, total[:n]).astype(BF16)
    down[...] = jnp.where(at[CORE] == 0, total[n:], total[n:] + far).astype(BF16)


def add(terms, first, depth, dtype, token):
    (out,), token = call(
        functools.partial(sum_kernel, first),
        [array((depth, terms[0].shape[1]), dtype)],
        [VMEM] * len(terms),
        terms,
        token,
    )
    return out, token


def body(grad_codes, grad_scales, weight_codes, weight_scales, gate_preact, up_preact):
    at = jnp.stack([lax.axis_index(a) for a in ("zh", "y", "x", "zl", "core")]).astype(jnp.int32)
    (own, mine), token = call(
        expand_kernel,
        [array(weight_codes.shape, BF16), array(grad_codes.shape[::-1], BF16)],
        [VMEM] * 4,
        (weight_codes, weight_scales, grad_codes, grad_scales),
    )
    weight = lax.all_gather(own, ("zh", "y"), axis=0, tiled=True)
    upstream = gather_upstream(mine, token)
    (hidden,), token = call(
        hidden_unit_kernel, [array(gate_preact.shape, BF16)], [VMEM, VMEM], (gate_preact, up_preact), token
    )

    depth, width = mine.shape
    terms = functools.partial(partials, at, hidden, upstream)
    (far2, far1), token = terms([[(2, 2)], [(1, 2), (3, 2)]], [BF16, BF16], token)
    far2, far1 = send_split(far2, "y"), send_split(far1, "y")
    (right2, left2, here2), token = terms([[(2, jy)] for jy in (1, 3, 0)], [F32] * 3, token)
    (right1, left1, here1), token = terms([[(1, jy), (3, jy)] for jy in (1, 3, 0)], [F32] * 3, token)
    (right2, left2), token = spread(at, right2, left2, far2, token)
    right2, left2 = send(right2, "y", 1), send(left2, "y", -1)
    (right1, left1), token = spread(at, right1, left1, far1, token)
    right1, left1 = send(right1, "y", 1), send(left1, "y", -1)
    (far0, right0, left0, here0), token = terms([[(0, jy)] for jy in (2, 1, 3, 0)], [BF16, F32, F32, F32], token)
    far0 = send_split(far0, "y")
    sum2, token = add([here2, right2, left2], [0] * 3, depth, BF16, token)
    sum2 = send_split(sum2, "zh")
    (right0, left0), token = spread(at, right0, left0, far0, token)
    right0, left0 = send(right0, "y", 1), send(left0, "y", -1)
    (sum1, sum3), token = call(
        sums_kernel, [array((depth, hidden.shape[1]), BF16)] * 2, [SMEM] + [VMEM] * 4, (at, here1, right1, left1, sum2), token
    )
    sum1, sum3 = send(sum1, "zh", 1), send(sum3, "zh", -1)
    (gate_grad, up_grad), token = hidden_grads(at, upstream, weight, gate_preact, up_preact, token)
    weight_grad, _ = add([here0, right0, left0, sum1, sum3], [0] * 5, depth, F32, token)
    return (gate_grad, up_grad, weight_grad)


def solution(mesh):
    fine = Mesh(mesh.devices.reshape(tuple(SIZE.values())), tuple(SIZE))
    dom, rep = ("zh", "y"), ("x", "zl", "core")
    in_specs = (P(dom, rep), P(rep, dom), P(dom, rep), P(dom, rep), P(dom, rep), P(dom, rep))
    out_specs = (P(dom, rep), P(dom, rep), P(dom, rep))
    return jax.shard_map(body, mesh=fine, in_specs=in_specs, out_specs=out_specs, check_vma=False)
```

```python
import functools

import jax
import jax.numpy as jnp
from jax import lax
from jax.experimental import pallas as pl
from jax.experimental.pallas import tpu as pltpu
from jax.sharding import Mesh
from jax.sharding import PartitionSpec as P

QB = 128
WHOLE = 58 * 1024 * 1024
SMALL = 16 * 1024 * 1024
ANY = pl.BlockSpec(memory_space=pl.ANY)
HBM = pl.BlockSpec(memory_space=pltpu.HBM)
SMEM = pl.BlockSpec(memory_space=pltpu.SMEM)
VMEM = pl.BlockSpec(memory_space=pltpu.VMEM)
SIZE = {"zh": 4, "y": 4, "x": 4, "zl": 2, "core": 2}
F32, BF16 = jnp.float32, jnp.bfloat16


def send(v, axis, step):
    n = SIZE[axis]
    return lax.ppermute(v, axis, [(i, (i + step) % n) for i in range(n)])


def call(kernel, shapes, in_specs, args, token=None, scratch=(), flops=0, moved=1 << 20, limit=SMALL, out_space=VMEM):
    tokens = () if token is None else token if isinstance(token, tuple) else (token,)
    n, m = len(args), len(shapes)

    def run(*refs):
        ins, rest = refs[:n], refs[n + len(tokens) :]
        rest[m][...] = jnp.zeros((8, 128), F32)
        kernel(*ins, *rest[:m], *rest[m + 1 :])

    out = pl.pallas_call(
        run,
        out_shape=[*shapes, array((8, 128), F32)],
        in_specs=[*in_specs, *[HBM] * len(tokens)],
        out_specs=[out_space] * m + [VMEM],
        scratch_shapes=list(scratch),
        compiler_params=pltpu.CompilerParams(vmem_limit_bytes=limit),
        cost_estimate=pl.CostEstimate(flops=flops, bytes_accessed=moved, transcendentals=0),
    )(*args, *tokens)
    return out[:-1], out[-1]


def array(shape, dtype):
    return jax.ShapeDtypeStruct(shape, dtype)


def expand_kernel(at, grad_codes, grad_scales, codes, scales, grad_out, out, *scratch):
    sems = scratch[-1]
    copies = [
        pltpu.make_async_copy(a, b, sems.at[i])
        for i, (a, b) in enumerate(zip((grad_codes, grad_scales, codes, scales), scratch))
    ]
    for c in copies:
        c.start()
    grad_codes, grad_scales, codes, scales = scratch[:-1]
    blocks = [slice(b * QB, (b + 1) * QB) for b in range(scales.shape[0])]
    copies[0].wait()
    copies[1].wait()
    for b, rows in enumerate(blocks):
        grad_out[rows, :] = (grad_codes[:, rows].astype(F32).T * grad_scales[b : b + 1, :]).astype(BF16)
    copies[2].wait()
    copies[3].wait()
    for b, rows in enumerate(blocks):
        out[rows, :] = (codes[rows, :].astype(F32) * scales[b : b + 1, :]).astype(BF16)


def hidden_unit_kernel(gate, up, out):
    g = gate[...].astype(F32)
    out[...] = (g * (1.0 / (1.0 + jnp.exp(-g))) * up[...].astype(F32)).astype(BF16)


def send_split(v, axis):
    n = SIZE[axis]
    return lax.ppermute(v, (axis, "core"), [(2 * i + c, 2 * ((i + 1 - 2 * c) % n) + c) for i in range(n) for c in range(2)])


ZH, Y, X, ZL, CORE = range(5)


def join_kernel(a, b, out):
    n = a.shape[0]
    out[:n, :] = a[...]
    out[n:, :] = b[...]


def gather_upstream(mine, token, meanwhile):
    depth, width = mine.shape
    pieces = []
    for zl, base in enumerate((mine, send(mine, "zl", 1))):
        swapped = send(base, "core", 1)
        (pair,), token = call(join_kernel, [array((2 * depth, width), BF16)], [VMEM] * 2, (base, swapped), token)
        near = send_split(pair, "x")
        if zl == 0:
            (result,), token = meanwhile(token)
            token = token, near
        other = send(near, "core", 1)
        far = send_split(near[:depth], "x")
        pieces += [(0, zl, 0, 0, pair), (0, zl, 1, depth, pair), (1, zl, 0, 0, near), (1, zl, 1, depth, near)]
        pieces += [(2, zl, 1, 0, other), (2, zl, 0, depth, other), (3, zl, 0, 0, far), (3, zl, 1, 0, send(far, "core", 1))]
    return pieces, result, token


def x_away(at, kind):
    return (0, 3 - 2 * at[CORE], 1 + 2 * at[CORE], 2)[kind]


def partial_kernel(plan, metas, at, hidden_ref, *refs):
    n = len(metas)
    m = len(plan)
    pieces, outs, done = refs[:n], refs[n : n + m], refs[n + m : n + 2 * m]
    held, hidden, sems, out_sems, hidden_sem = refs[n + 2 * m :]
    load = pltpu.make_async_copy(hidden_ref, hidden, hidden_sem)
    load.start()
    blocks = [b for group in plan for b in group]
    depth = held.shape[1]

    for i, (jz, jy) in enumerate(blocks):
        away, owner = lax.rem(at[ZH] + jz + 4 - at[X], 4), lax.rem(at[Y] + jy, 4)
        zl, core = jnp.bitwise_xor(lax.div(owner, 2), at[ZL]), jnp.bitwise_xor(lax.rem(owner, 2), at[CORE])
        for (kind, pzl, pcore, row), ref in zip(metas, pieces):

            @pl.when((away == x_away(at, kind)) & (zl == pzl) & (core == pcore))
            def _():
                pltpu.make_async_copy(ref.at[pl.ds(row, depth)], held.at[i], sems.at[i]).start()

    load.wait()
    copies = []
    for group, out, total in zip(plan, outs, done):
        for k in range(len(group)):
            i = len(copies)
            pltpu.make_async_copy(pieces[0].at[pl.ds(0, depth)], held.at[i], sems.at[i]).wait()
            r = jnp.dot(held[i], hidden[...], preferred_element_type=F32)
            rows = pl.ds(k * depth, depth)
            total[rows, :] = r.astype(out.dtype)
            copies.append(pltpu.make_async_copy(total.at[rows], out.at[rows], out_sems.at[i]))
            copies[-1].start()
    for c in copies:
        c.wait()


def partials(at, hidden, upstream, plan, dtypes, token):
    depth = upstream[0][-1].shape[0] // 2
    width = hidden.shape[1]
    n = sum(map(len, plan))
    shapes = [array((len(g) * depth, width), t) for g, t in zip(plan, dtypes)]
    return call(
        functools.partial(partial_kernel, plan, [p[:4] for p in upstream]),
        shapes,
        [SMEM, ANY] + [HBM] * len(upstream),
        (at, hidden, *[p[-1] for p in upstream]),
        token,
        [pltpu.VMEM(t.shape, t.dtype) for t in shapes]
        + [pltpu.VMEM((n, depth, hidden.shape[0]), BF16), pltpu.VMEM(hidden.shape, BF16)]
        + [pltpu.SemaphoreType.DMA((n,)), pltpu.SemaphoreType.DMA((n,)), pltpu.SemaphoreType.DMA],
        2 * hidden.shape[0] * width * depth * n,
        4 * 1024 * 1024,
        24 * 1024 * 1024,
        HBM,
    )


TILE = 448


def hidden_kernel(metas, at, weight, gate, up, *refs):
    n = len(metas)
    pieces = refs[:n]
    gate_out, up_out, uheld, wheld, sem = refs[n:]
    depth = uheld.shape[0] // 16

    def copies():
        yield pltpu.make_async_copy(weight, wheld, sem)
        for (kind, zl, core, row), ref in zip(metas, pieces):
            x = lax.rem(at[X] + x_away(at, kind), 4)
            f = 4 * x + 2 * jnp.bitwise_xor(at[ZL], zl) + jnp.bitwise_xor(at[CORE], core)
            rows = pl.ds(pl.multiple_of(f * depth, depth), depth)
            yield pltpu.make_async_copy(ref.at[pl.ds(row, depth)], uheld.at[rows], sem)

    for c in copies():
        c.start()
    for c in copies():
        c.wait()

    for i in range(gate.shape[0] // TILE):
        rows = slice(i * TILE, (i + 1) * TILE)
        grad = lax.dot_general(uheld[:, rows], wheld[...], (((0,), (0,)), ((), ())), preferred_element_type=F32)
        g = gate[rows, :].astype(F32)
        u = up[rows, :].astype(F32)
        s = 1.0 / (1.0 + jnp.exp(-g))
        up_out[rows, :] = (grad * (g * s)).astype(BF16)
        gate_out[rows, :] = (grad * u * s * (1.0 + g * (1.0 - s))).astype(BF16)


def hidden_grads(at, upstream, weight, gate, up, token):
    return call(
        functools.partial(hidden_kernel, [p[:4] for p in upstream]),
        [array(gate.shape, BF16)] * 2,
        [SMEM, HBM, VMEM, VMEM] + [HBM] * len(upstream),
        (at, weight, gate, up, *[p[-1] for p in upstream]),
        token,
        [pltpu.VMEM(weight.shape, BF16), pltpu.VMEM(weight.shape, BF16), pltpu.SemaphoreType.DMA],
        2 * gate.shape[0] * gate.shape[1] * weight.shape[0],
        20 * 1024 * 1024,
        WHOLE,
    )


def spread_kernel(at, right, left, far, to_right, to_left):
    to_right[...] = right[...].astype(BF16)
    to_left[...] = left[...].astype(BF16)

    @pl.when(at[CORE] == 0)
    def _():
        to_right[...] = (right[...] + far[...].astype(F32)).astype(BF16)

    @pl.when(at[CORE] != 0)
    def _():
        to_left[...] = (left[...] + far[...].astype(F32)).astype(BF16)


def spread(at, right, left, far, token):
    return call(spread_kernel, [array(right.shape, BF16)] * 2, [SMEM, VMEM, VMEM, VMEM], (at, right, left, far), token)


def sum_kernel(first, *refs):
    out = refs[-1]
    rows = out.shape[0]
    total = 0.0
    for start, ref in zip(first, refs):
        total = total + ref[start : start + rows, :].astype(F32)
    out[...] = total.astype(out.dtype)


def sums_kernel(at, here, right, left, far, right0, left0, far0, up, down, to_right, to_left):
    n = up.shape[0]
    far = far[...].astype(F32)
    total = here[...] + right[...].astype(F32) + left[...].astype(F32)
    up[...] = jnp.where(at[CORE] == 0, total[:n] + far, total[:n]).astype(BF16)
    down[...] = jnp.where(at[CORE] == 0, total[n:], total[n:] + far).astype(BF16)
    spread_kernel(at, right0, left0, far0, to_right, to_left)


def add(terms, first, depth, dtype, token):
    (out,), token = call(
        functools.partial(sum_kernel, first),
        [array((depth, terms[0].shape[1]), dtype)],
        [VMEM] * len(terms),
        terms,
        token,
    )
    return out, token


def body(grad_codes, grad_scales, weight_codes, weight_scales, gate_preact, up_preact):
    at = jnp.stack([lax.axis_index(a) for a in ("zh", "y", "x", "zl", "core")]).astype(jnp.int32)
    quantized = (grad_codes, grad_scales, weight_codes, weight_scales)
    (mine, own), token = call(
        expand_kernel,
        [array(grad_codes.shape[::-1], BF16), array(weight_codes.shape, BF16)],
        [SMEM] + [ANY] * 4,
        (at, *quantized),
        scratch=[pltpu.VMEM(q.shape, q.dtype) for q in quantized] + [pltpu.SemaphoreType.DMA((4,))],
        limit=WHOLE,
    )
    weight = lax.all_gather(own, ("zh", "y"), axis=0, tiled=True)

    def units(token):
        return call(hidden_unit_kernel, [array(gate_preact.shape, BF16)], [VMEM, VMEM], (gate_preact, up_preact), token)

    upstream, hidden, token = gather_upstream(mine, token, units)

    depth, width = mine.shape[0], hidden.shape[1]
    terms = functools.partial(partials, at, hidden, upstream)
    (far2, far1), token = terms([[(2, 2)], [(1, 2), (3, 2)]], [BF16, BF16], token)
    far2, far1 = send_split(far2, "y"), send_split(far1, "y")
    (right2, left2, here2), token = terms([[(2, jy)] for jy in (1, 3, 0)], [F32] * 3, token)
    (right1, left1, here1), token = terms([[(1, jy), (3, jy)] for jy in (1, 3, 0)], [F32] * 3, token)
    (right2, left2), token = spread(at, right2, left2, far2, token)
    right2, left2 = send(right2, "y", 1), send(left2, "y", -1)
    (right1, left1), token = spread(at, right1, left1, far1, token)
    right1, left1 = send(right1, "y", 1), send(left1, "y", -1)
    (far0, right0, left0, here0), token = terms([[(0, jy)] for jy in (2, 1, 3, 0)], [BF16, F32, F32, F32], token)
    far0 = send_split(far0, "y")
    sum2, token = add([here2, right2, left2], [0] * 3, depth, BF16, token)
    sum2 = send_split(sum2, "zh")
    (gate_grad, up_grad), token = hidden_grads(at, upstream, weight, gate_preact, up_preact, token)
    (sum1, sum3, right0, left0), token = call(
        sums_kernel,
        [array((depth, width), BF16)] * 4,
        [SMEM] + [VMEM] * 7,
        (at, here1, right1, left1, sum2, right0, left0, far0),
        token,
    )
    sum1, sum3 = send(sum1, "zh", 1), send(sum3, "zh", -1)
    right0, left0 = send(right0, "y", 1), send(left0, "y", -1)
    weight_grad, _ = add([here0, right0, left0, sum1, sum3], [0] * 5, depth, F32, token)
    return (gate_grad, up_grad, weight_grad)


def solution(mesh):
    fine = Mesh(mesh.devices.reshape(tuple(SIZE.values())), tuple(SIZE))
    dom, rep = ("zh", "y"), ("x", "zl", "core")
    in_specs = (P(dom, rep), P(rep, dom), P(dom, rep), P(dom, rep), P(dom, rep), P(dom, rep))
    out_specs = (P(dom, rep), P(dom, rep), P(dom, rep))
    return jax.shard_map(body, mesh=fine, in_specs=in_specs, out_specs=out_specs, check_vma=False)
```

```python
import functools

import jax
import jax.numpy as jnp
from jax import lax
from jax.experimental import pallas as pl
from jax.experimental.pallas import tpu as pltpu
from jax.sharding import Mesh
from jax.sharding import PartitionSpec as P

QB = 128
WHOLE = 58 * 1024 * 1024
SMALL = 16 * 1024 * 1024
ANY = pl.BlockSpec(memory_space=pl.ANY)
HBM = pl.BlockSpec(memory_space=pltpu.HBM)
SMEM = pl.BlockSpec(memory_space=pltpu.SMEM)
VMEM = pl.BlockSpec(memory_space=pltpu.VMEM)
SIZE = {"zh": 4, "y": 4, "x": 4, "zl": 2, "core": 2}
F32, BF16 = jnp.float32, jnp.bfloat16


def send(v, axis, step):
    n = SIZE[axis]
    return lax.ppermute(v, axis, [(i, (i + step) % n) for i in range(n)])


def call(kernel, shapes, in_specs, args, token=None, scratch=(), flops=0, moved=1 << 20, limit=SMALL, out_space=VMEM, aliases=None):
    tokens = () if token is None else token if isinstance(token, tuple) else (token,)
    n, m = len(args), len(shapes)

    def run(*refs):
        ins, rest = refs[:n], refs[n + len(tokens) :]
        rest[m][...] = jnp.zeros((8, 128), F32)
        kernel(*ins, *rest[:m], *rest[m + 1 :])

    out = pl.pallas_call(
        run,
        out_shape=[*shapes, array((8, 128), F32)],
        in_specs=[*in_specs, *[HBM] * len(tokens)],
        out_specs=[out_space] * m + [VMEM],
        scratch_shapes=list(scratch),
        input_output_aliases=aliases or {},
        compiler_params=pltpu.CompilerParams(vmem_limit_bytes=limit),
        cost_estimate=pl.CostEstimate(flops=flops, bytes_accessed=moved, transcendentals=0),
    )(*args, *tokens)
    return out[:-1], out[-1]


def array(shape, dtype):
    return jax.ShapeDtypeStruct(shape, dtype)


def expand_kernel(at, grad_codes, grad_scales, codes, scales, grad_out, out, *scratch):
    sems = scratch[-1]
    copies = [
        pltpu.make_async_copy(a, b, sems.at[i])
        for i, (a, b) in enumerate(zip((grad_codes, grad_scales, codes, scales), scratch))
    ]
    for c in copies:
        c.start()
    grad_codes, grad_scales, codes, scales = scratch[:-1]
    blocks = [slice(b * QB, (b + 1) * QB) for b in range(scales.shape[0])]
    copies[0].wait()
    copies[1].wait()
    for b, rows in enumerate(blocks):
        grad_out[rows, :] = (grad_codes[:, rows].astype(F32).T * grad_scales[b : b + 1, :]).astype(BF16)
    copies[2].wait()
    copies[3].wait()
    for b, rows in enumerate(blocks):
        out[rows, :] = (codes[rows, :].astype(F32) * scales[b : b + 1, :]).astype(BF16)


def hidden_unit_kernel(gate, up, out):
    g = gate[...].astype(F32)
    out[...] = (g * (1.0 / (1.0 + jnp.exp(-g))) * up[...].astype(F32)).astype(BF16)


def send_split(v, axis):
    n = SIZE[axis]
    return lax.ppermute(v, (axis, "core"), [(2 * i + c, 2 * ((i + 1 - 2 * c) % n) + c) for i in range(n) for c in range(2)])


ZH, Y, X, ZL, CORE = range(5)


def join_kernel(a, b, out):
    n = a.shape[0]
    out[:n, :] = a[...]
    out[n:, :] = b[...]


def gather_upstream(mine, token, meanwhile):
    depth, width = mine.shape
    pieces = []
    for zl, base in enumerate((mine, send(mine, "zl", 1))):
        swapped = send(base, "core", 1)
        (pair,), token = call(join_kernel, [array((2 * depth, width), BF16)], [VMEM] * 2, (base, swapped), token)
        near = send_split(pair, "x")
        if zl == 0:
            (result,), token = meanwhile(token)
            token = token, near
        other = send(near, "core", 1)
        far = send_split(near[:depth], "x")
        pieces += [(0, zl, 0, 0, pair), (0, zl, 1, depth, pair), (1, zl, 0, 0, near), (1, zl, 1, depth, near)]
        pieces += [(2, zl, 1, 0, other), (2, zl, 0, depth, other), (3, zl, 0, 0, far), (3, zl, 1, 0, send(far, "core", 1))]
    return pieces, result, token


def x_away(at, kind):
    return (0, 3 - 2 * at[CORE], 1 + 2 * at[CORE], 2)[kind]


def partial_kernel(plan, metas, at, hidden_ref, *refs):
    n = len(metas)
    m = len(plan)
    pieces, outs, done = refs[:n], refs[n : n + m], refs[n + m : n + 2 * m]
    held, hidden, sems, out_sems, hidden_sem = refs[n + 2 * m :]
    load = pltpu.make_async_copy(hidden_ref, hidden, hidden_sem)
    load.start()
    blocks = [b for group in plan for b in group]
    depth = held.shape[1]

    for i, (jz, jy) in enumerate(blocks):
        away, owner = lax.rem(at[ZH] + jz + 4 - at[X], 4), lax.rem(at[Y] + jy, 4)
        zl, core = jnp.bitwise_xor(lax.div(owner, 2), at[ZL]), jnp.bitwise_xor(lax.rem(owner, 2), at[CORE])
        for (kind, pzl, pcore, row), ref in zip(metas, pieces):

            @pl.when((away == x_away(at, kind)) & (zl == pzl) & (core == pcore))
            def _():
                pltpu.make_async_copy(ref.at[pl.ds(row, depth)], held.at[i], sems.at[i]).start()

    load.wait()
    copies = []
    for group, out, total in zip(plan, outs, done):
        for k in range(len(group)):
            i = len(copies)
            pltpu.make_async_copy(pieces[0].at[pl.ds(0, depth)], held.at[i], sems.at[i]).wait()
            r = jnp.dot(held[i], hidden[...], preferred_element_type=F32)
            rows = pl.ds(k * depth, depth)
            total[rows, :] = r.astype(out.dtype)
            copies.append(pltpu.make_async_copy(total.at[rows], out.at[rows], out_sems.at[i]))
            copies[-1].start()
    for c in copies:
        c.wait()


def partials(at, hidden, upstream, plan, dtypes, token):
    depth = upstream[0][-1].shape[0] // 2
    width = hidden.shape[1]
    n = sum(map(len, plan))
    shapes = [array((len(g) * depth, width), t) for g, t in zip(plan, dtypes)]
    return call(
        functools.partial(partial_kernel, plan, [p[:4] for p in upstream]),
        shapes,
        [SMEM, ANY] + [HBM] * len(upstream),
        (at, hidden, *[p[-1] for p in upstream]),
        token,
        [pltpu.VMEM(t.shape, t.dtype) for t in shapes]
        + [pltpu.VMEM((n, depth, hidden.shape[0]), BF16), pltpu.VMEM(hidden.shape, BF16)]
        + [pltpu.SemaphoreType.DMA((n,)), pltpu.SemaphoreType.DMA((n,)), pltpu.SemaphoreType.DMA],
        2 * hidden.shape[0] * width * depth * n,
        4 * 1024 * 1024,
        24 * 1024 * 1024,
        HBM,
    )


def hidden_kernel(metas, first, at, weight, gate, up, *refs):
    n = len(metas)
    pieces = refs[:n]
    gate_out, up_out, uheld, wheld, gate_held, up_held, gate_done, up_done, sem, sems = refs[-10:]
    depth, tokens = uheld.shape[0] // 16, uheld.shape[1]
    mine = pl.ds(first, tokens)

    def copies():
        yield pltpu.make_async_copy(weight, wheld, sem)
        yield pltpu.make_async_copy(gate.at[mine], gate_held, sem)
        yield pltpu.make_async_copy(up.at[mine], up_held, sem)
        for (kind, zl, core, row), ref in zip(metas, pieces):
            x = lax.rem(at[X] + x_away(at, kind), 4)
            f = 4 * x + 2 * jnp.bitwise_xor(at[ZL], zl) + jnp.bitwise_xor(at[CORE], core)
            rows = pl.ds(pl.multiple_of(f * depth, depth), depth)
            yield pltpu.make_async_copy(ref.at[pl.ds(row, depth), mine], uheld.at[rows], sem)

    for c in copies():
        c.start()
    for c in copies():
        c.wait()

    tile = 256 if tokens % 256 == 0 else 128
    for i in range(tokens // tile):
        rows = slice(i * tile, (i + 1) * tile)
        grad = lax.dot_general(uheld[:, rows], wheld[...], (((0,), (0,)), ((), ())), preferred_element_type=F32)
        g = gate_held[rows, :].astype(F32)
        u = up_held[rows, :].astype(F32)
        s = 1.0 / (1.0 + jnp.exp(-g))
        up_done[rows, :] = (grad * (g * s)).astype(BF16)
        gate_done[rows, :] = (grad * u * s * (1.0 + g * (1.0 - s))).astype(BF16)
    outs = [
        pltpu.make_async_copy(gate_done, gate_out.at[mine], sems.at[0]),
        pltpu.make_async_copy(up_done, up_out.at[mine], sems.at[1]),
    ]
    for c in outs:
        c.start()
    for c in outs:
        c.wait()


def hidden_grads(at, upstream, weight, gate, up, token, first, tokens, into=()):
    args = (at, weight, gate, up, *[p[-1] for p in upstream], *into)
    width = gate.shape[1]
    return call(
        functools.partial(hidden_kernel, [p[:4] for p in upstream], first),
        [array(gate.shape, BF16)] * 2,
        [SMEM] + [ANY] * (len(args) - 1),
        args,
        token,
        [pltpu.VMEM((weight.shape[0], tokens), BF16), pltpu.VMEM(weight.shape, BF16)]
        + [pltpu.VMEM((tokens, width), BF16)] * 4
        + [pltpu.SemaphoreType.DMA, pltpu.SemaphoreType.DMA((2,))],
        2 * tokens * width * weight.shape[0],
        20 * 1024 * 1024,
        WHOLE,
        ANY,
        {len(args) - 2: 0, len(args) - 1: 1} if into else None,
    )


def spread_kernel(at, right, left, far, to_right, to_left):
    to_right[...] = right[...].astype(BF16)
    to_left[...] = left[...].astype(BF16)

    @pl.when(at[CORE] == 0)
    def _():
        to_right[...] = (right[...] + far[...].astype(F32)).astype(BF16)

    @pl.when(at[CORE] != 0)
    def _():
        to_left[...] = (left[...] + far[...].astype(F32)).astype(BF16)


def spread(at, right, left, far, token):
    return call(spread_kernel, [array(right.shape, BF16)] * 2, [SMEM, VMEM, VMEM, VMEM], (at, right, left, far), token)


def sum_kernel(first, *refs):
    out = refs[-1]
    rows = out.shape[0]
    total = 0.0
    for start, ref in zip(first, refs):
        total = total + ref[start : start + rows, :].astype(F32)
    out[...] = total.astype(out.dtype)


def sums_kernel(at, here, right, left, far, far0, up, down, far0_out):
    n = up.shape[0]
    far = far[...].astype(F32)
    total = here[...] + right[...].astype(F32) + left[...].astype(F32)
    up[...] = jnp.where(at[CORE] == 0, total[:n] + far, total[:n]).astype(BF16)
    down[...] = jnp.where(at[CORE] == 0, total[n:], total[n:] + far).astype(BF16)
    far0_out[...] = far0[...]


def add(terms, first, depth, dtype, token):
    (out,), token = call(
        functools.partial(sum_kernel, first),
        [array((depth, terms[0].shape[1]), dtype)],
        [VMEM] * len(terms),
        terms,
        token,
    )
    return out, token


def body(grad_codes, grad_scales, weight_codes, weight_scales, gate_preact, up_preact):
    at = jnp.stack([lax.axis_index(a) for a in ("zh", "y", "x", "zl", "core")]).astype(jnp.int32)
    quantized = (grad_codes, grad_scales, weight_codes, weight_scales)
    (mine, own), token = call(
        expand_kernel,
        [array(grad_codes.shape[::-1], BF16), array(weight_codes.shape, BF16)],
        [SMEM] + [ANY] * 4,
        (at, *quantized),
        scratch=[pltpu.VMEM(q.shape, q.dtype) for q in quantized] + [pltpu.SemaphoreType.DMA((4,))],
        limit=WHOLE,
    )
    weight = lax.all_gather(own, ("zh", "y"), axis=0, tiled=True)

    def units(token):
        return call(hidden_unit_kernel, [array(gate_preact.shape, BF16)], [VMEM, VMEM], (gate_preact, up_preact), token)

    upstream, hidden, token = gather_upstream(mine, token, units)

    depth, width = mine.shape[0], hidden.shape[1]
    terms = functools.partial(partials, at, hidden, upstream)
    (far2, far1), token = terms([[(2, 2)], [(1, 2), (3, 2)]], [BF16, BF16], token)
    far2, far1 = send_split(far2, "y"), send_split(far1, "y")
    (right2, left2, here2), token = terms([[(2, jy)] for jy in (1, 3, 0)], [F32] * 3, token)
    (right1, left1, here1), token = terms([[(1, jy), (3, jy)] for jy in (1, 3, 0)], [F32] * 3, token)
    (right2, left2), token = spread(at, right2, left2, far2, token)
    right2, left2 = send(right2, "y", 1), send(left2, "y", -1)
    (right1, left1), token = spread(at, right1, left1, far1, token)
    right1, left1 = send(right1, "y", 1), send(left1, "y", -1)
    (far0, right0, left0, here0), token = terms([[(0, jy)] for jy in (2, 1, 3, 0)], [BF16, F32, F32, F32], token)
    sum2, token = add([here2, right2, left2], [0] * 3, depth, BF16, token)
    sum2 = send_split(sum2, "zh")
    tokens = gate_preact.shape[0]
    cut = -(-tokens // 256) * 128
    grads, token = hidden_grads(at, upstream, weight, gate_preact, up_preact, token, 0, cut)
    (sum1, sum3, far0), token = call(
        sums_kernel,
        [array((depth, width), BF16)] * 3,
        [SMEM] + [VMEM] * 5,
        (at, here1, right1, left1, sum2, far0),
        token,
    )
    sum1, sum3 = send(sum1, "zh", 1), send(sum3, "zh", -1)
    (right0, left0), token = spread(at, right0, left0, send_split(far0, "y"), token)
    right0, left0 = send(right0, "y", 1), send(left0, "y", -1)
    (gate_grad, up_grad), token = hidden_grads(
        at, upstream, weight, gate_preact, up_preact, token, cut, tokens - cut, grads
    )
    weight_grad, token = add([here0, sum1, sum3], [0] * 3, depth, F32, token)
    weight_grad, _ = add([weight_grad, right0, left0], [0] * 3, depth, F32, token)
    return (gate_grad, up_grad, weight_grad)


def solution(mesh):
    fine = Mesh(mesh.devices.reshape(tuple(SIZE.values())), tuple(SIZE))
    dom, rep = ("zh", "y"), ("x", "zl", "core")
    in_specs = (P(dom, rep), P(rep, dom), P(dom, rep), P(dom, rep), P(dom, rep), P(dom, rep))
    out_specs = (P(dom, rep), P(dom, rep), P(dom, rep))
    return jax.shard_map(body, mesh=fine, in_specs=in_specs, out_specs=out_specs, check_vma=False)
```
